256 devices in a mesh: row: 32 (over x, y, core), col: 8 (over z).
Axes of the slice: x: 4, y: 4, z: 8, core: 2. Of those that a mesh axis runs over, the one named last changes fastest.
Arguments:
- inputs: bfloat16 [512, 12288], P('col', 'row'), may hold values from -6 to 6
- weight: bfloat16 [12288, 49152], P('row', 'col'), may hold values from -0.0546875 to 0.0546875
- grad_out: bfloat16 [512, 49152], P('row', 'col'), may hold values from -1.5 to 1.5
Outputs:
- projected: bfloat16 [512, 49152], P('row', 'col')
- grad_inputs: bfloat16 [512, 12288], P('col', 'row')
- grad_weight: bfloat16 [12288, 49152], P('row', 'col')
The draws below stay inside these ranges and needn't reach their ends.
All inputs are finite; a program needn't handle non-finite values.
Results may differ from the reference program's by a relative error of at most 0.001.
Values may be sent and summed in bfloat16 or wider, within the bound.
No kernel may reach another device: no remote copies, remote signals or barrier semaphores. Data moves between devices by JAX's collectives and lax.ppermute only.
A program may use at most 128 MiB of HBM per device.

```python
import jax
import jax.numpy as jnp
from jax import lax

D = 12288
FF = 49152
TOKENS = 512


def shard_levels(stream_key, shape, split, least, largest):
    level = 1.0
    for position, blocks in split:
        heights = jax.random.uniform(jax.random.fold_in(jax.random.fold_in(stream_key, 6), position), (blocks,), jnp.float32, least / len(split), largest / len(split))
        level = level * jnp.repeat(jnp.exp(heights), shape[position] // blocks).reshape((-1,) + (1,) * (len(shape) - 1 - position))
    return level


def scatter_about(own_key, dims, deviation, bound, cuts=(), dtype=jnp.bfloat16):
    factor_of = shard_levels(own_key, dims, cuts, -0.22, 0.18) if cuts else 1.0
    drawn = jax.random.normal(own_key, dims, jnp.float32) * deviation * factor_of
    return jnp.minimum(jnp.maximum(drawn, -bound), bound).astype(dtype)


def setup_inputs(seed: int = 0) -> dict:
    key_of = jax.random.split(jax.random.key(seed), 4)
    inputs = scatter_about(key_of[0], (TOKENS, D), 1.0, 6.0, ((0, 8), (1, 32)))
    weight = scatter_about(key_of[1], (D, FF), D ** -0.5, 0.0546875, ((0, 32), (1, 8)))
    grad_out = scatter_about(key_of[2], (TOKENS, FF), 0.25, 1.5, ((0, 32), (1, 8)))
    return dict(inputs=inputs, weight=weight, grad_out=grad_out)


def reference(inputs, weight, grad_out):
    projected = jnp.dot(inputs, weight, preferred_element_type=jnp.float32).astype(jnp.bfloat16)
    grad_inputs = lax.dot_general(grad_out, weight, (((1,), (1,)), ((), ())), preferred_element_type=jnp.float32).astype(jnp.bfloat16)
    grad_weight = lax.dot_general(inputs, grad_out, (((0,), (0,)), ((), ())), preferred_element_type=jnp.float32).astype(jnp.bfloat16)
    return projected, grad_inputs, grad_weight
```

```python
import functools

import jax
import jax.numpy as jnp
from jax import lax
from jax.experimental import pallas as pl
from jax.experimental.pallas import tpu as pltpu
from jax.sharding import Mesh, PartitionSpec as P

BF = jnp.bfloat16
F32 = jnp.float32
SPAN = 86.5
LANES = 128
STEPS = (1, 3, 2)


def get(value, axis, distance):
    return lax.ppermute(value, axis, [((i + distance) % 4, i) for i in range(4)])


def swap(value):
    return lax.ppermute(value, "core", [(0, 1), (1, 0)])


def encode(block):
    size = jnp.abs(block)
    top = jnp.maximum(jnp.max(size, axis=0, keepdims=True), 1e-30)
    top = (top * (1.0 + 2.0**-7)).astype(BF).astype(F32)
    level = jnp.exp(size * (2 * SPAN / top) - SPAN)
    return jnp.where(block < 0, -level, level).astype(BF), top


def decode(code, top):
    code = code.astype(F32)
    size = (jnp.log(jnp.abs(code)) + SPAN) * (top / (2 * SPAN))
    return jnp.where(code < 0, -size, size)


def block_of(pos, dx, dy, core):
    return (((pos[0] + dx) % 4) * 4 + (pos[1] + dy) % 4) * 2 + core


def rows_of(index):
    return pl.ds(pl.multiple_of(index * 16, 16), 16)


def project_kernel(half, pos, own_in, par_in, w_own, w_par, keep, out1, out2, out3, lo, lp, tops):
    j = pl.program_id(0)

    @pl.when(j == 0)
    def _():
        tops[...] = jnp.zeros_like(tops)
        for first in range(4):
            for second in range(4):
                dx, dy = (first, second) if half == 0 else (second, first)
                for core in range(2):
                    to = ((first * 4 + second) * 2 + core) * 16
                    rows = rows_of(block_of(pos, dx, dy, core))
                    lo[to : to + 16, :] = own_in[rows, :]
                    lp[to : to + 16, :] = par_in[rows, :]

    total = jnp.dot(lo[...], w_own[...], preferred_element_type=F32)
    total += jnp.dot(lp[...], w_par[...], preferred_element_type=F32)
    tiles = total.shape[1] // LANES
    for k in range(tiles):
        lanes = slice(k * LANES, (k + 1) * LANES)
        tile = j * tiles + k
        rows = pl.ds(pl.multiple_of(tile * 128, 128), 128)
        keep[rows, :] = total[:128, lanes]
        for p, out in enumerate((out1, out2, out3)):
            d = STEPS[p]
            code, top = encode(total[d * 128 : (d + 1) * 128, lanes])
            out[rows, :] = code
            tops[p, pl.ds(tile, 1), :] = top

    @pl.when(j == pl.num_programs(0) - 1)
    def _():
        for p, out in enumerate((out1, out2, out3)):
            out[1536:1552, :] = tops[p].astype(BF)


def project(half, pos, own_in, par_in, weight, weight_par):
    width = 512
    piece = jax.ShapeDtypeStruct((1552, LANES), BF)
    whole = lambda j, pos: (0, 0)
    return pl.pallas_call(
        functools.partial(project_kernel, half),
        grid_spec=pltpu.PrefetchScalarGridSpec(
            num_scalar_prefetch=1,
            grid=(3,),
            in_specs=[
                pl.BlockSpec((512, 384), whole),
                pl.BlockSpec((512, 384), whole),
                pl.BlockSpec((384, width), lambda j, pos: (0, pos[2] * 6 + half * 3 + j)),
                pl.BlockSpec((384, width), lambda j, pos: (0, half * 3 + j)),
            ],
            out_specs=[pl.BlockSpec((1536, LANES), whole)] + [pl.BlockSpec((1552, LANES), whole)] * 3,
            scratch_shapes=[
                pltpu.VMEM((512, 384), BF),
                pltpu.VMEM((512, 384), BF),
                pltpu.VMEM((3, 16, LANES), F32),
            ],
        ),
        out_shape=[jax.ShapeDtypeStruct((1536, LANES), F32), piece, piece, piece],
        compiler_params=pltpu.CompilerParams(vmem_limit_bytes=24 * 2**20),
        cost_estimate=pl.CostEstimate(flops=2 * 512 * 768 * 1536, bytes_accessed=5 * 2**20, transcendentals=2**19),
        name="project",
    )(pos, own_in, par_in, weight, weight_par)


def relay_kernel(own, in1, in2, in3, keep, out1, out2, out3, tops):
    tops[...] = jnp.zeros_like(tops)
    heads = [ref[1536:1552, :].astype(F32) for ref in (in1, in2, in3)]
    for j in range(12):
        rows = slice(j * 128, (j + 1) * 128)
        total = own[rows, :]
        for ref, head in zip((in1, in2, in3), heads):
            total += decode(ref[rows, :], head[j : j + 1, :])
        to = slice(j * 32, (j + 1) * 32)
        keep[to, :] = total[:32, :]
        for p, out in enumerate((out1, out2, out3)):
            d = STEPS[p]
            code, top = encode(total[d * 32 : (d + 1) * 32, :])
            out[to, :] = code
            tops[p, j : j + 1, :] = top
    for p, out in enumerate((out1, out2, out3)):
        out[384:400, :] = tops[p].astype(BF)


def relay(own, pieces):
    piece = jax.ShapeDtypeStruct((400, LANES), BF)
    return pl.pallas_call(
        relay_kernel,
        out_shape=[jax.ShapeDtypeStruct((384, LANES), F32), piece, piece, piece],
        scratch_shapes=[pltpu.VMEM((3, 16, LANES), F32)],
        compiler_params=pltpu.CompilerParams(vmem_limit_bytes=16 * 2**20),
        cost_estimate=pl.CostEstimate(flops=2**22, bytes_accessed=3 * 2**20, transcendentals=2**20),
        name="relay",
    )(own, *pieces)


def finish_kernel(pos, *refs):
    keep, send = refs[-2:]
    core = pos[2]
    for half in range(2):
        own, *ins = refs[half * 4 : half * 4 + 4]
        heads = [ref[384:400, :].astype(F32) for ref in ins]
        for j in range(12):
            rows = slice(j * 32, (j + 1) * 32)
            total = own[rows, :]
            for ref, head in zip(ins, heads):
                total += decode(ref[rows, :], head[j : j + 1, :])
            lanes = slice(half * 1536 + j * LANES, half * 1536 + (j + 1) * LANES)
            low, high = total[:16, :].astype(BF), total[16:, :].astype(BF)
            keep[:, lanes] = jnp.where(core == 0, low, high)
            send[:, lanes] = jnp.where(core == 0, high, low)


def finish(pos, *arrays):
    return pl.pallas_call(
        finish_kernel,
        in_specs=[pl.BlockSpec(memory_space=pltpu.SMEM)] + [pl.BlockSpec(memory_space=pltpu.VMEM)] * 8,
        out_shape=[jax.ShapeDtypeStruct((16, 3072), BF)] * 2,
        compiler_params=pltpu.CompilerParams(vmem_limit_bytes=16 * 2**20),
        cost_estimate=pl.CostEstimate(flops=2**20, bytes_accessed=2**20, transcendentals=2**18),
        name="finish",
    )(pos, *arrays)


CONTRACT_LAST = (((1,), (1,)), ((), ()))


def grad_inputs_kernel(pos, a_own, a_par, b_own, b_par, w_a, w_b, out, acc_a, acc_b):
    j = pl.program_id(0)
    terms = [
        lax.dot_general(cot[...], w[...], CONTRACT_LAST, preferred_element_type=F32)
        for cot, w in ((a_own, w_a), (a_par, w_a), (b_own, w_b), (b_par, w_b))
    ]

    @pl.when(j == 0)
    def _():
        acc_a[:256, :], acc_a[256:, :], acc_b[:256, :], acc_b[256:, :] = terms

    @pl.when(j > 0)
    def _():
        acc_a[:256, :] = acc_a[:256, :] + terms[0]
        acc_a[256:, :] = acc_a[256:, :] + terms[1]
        acc_b[:256, :] = acc_b[:256, :] + terms[2]
        acc_b[256:, :] = acc_b[256:, :] + terms[3]

    @pl.when(j == pl.num_programs(0) - 1)
    def _():
        for rel in range(2):
            core = pos[2] if rel == 0 else 1 - pos[2]
            for dx in range(4):
                for dy in range(4):
                    a = ((rel * 4 + dy) * 4 + dx) * 16
                    b = ((rel * 4 + dx) * 4 + dy) * 16
                    out[rows_of(block_of(pos, dx, dy, core)), :] = acc_a[a : a + 16, :] + acc_b[b : b + 16, :]


def grad_inputs_terms(pos, a_own, a_par, b_own, b_par, weight):
    width = 512
    part = lambda j, pos: (0, j)
    return pl.pallas_call(
        grad_inputs_kernel,
        grid_spec=pltpu.PrefetchScalarGridSpec(
            num_scalar_prefetch=1,
            grid=(6,),
            in_specs=[pl.BlockSpec((256, width), part)] * 4
            + [pl.BlockSpec((384, width), part), pl.BlockSpec((384, width), lambda j, pos: (0, j + 6))],
            out_specs=pl.BlockSpec((512, 384), lambda j, pos: (0, 0)),
            scratch_shapes=[pltpu.VMEM((512, 384), F32), pltpu.VMEM((512, 384), F32)],
        ),
        out_shape=jax.ShapeDtypeStruct((512, 384), F32),
        compiler_params=pltpu.CompilerParams(vmem_limit_bytes=24 * 2**20),
        cost_estimate=pl.CostEstimate(flops=2 * 512 * 384 * 6144, bytes_accessed=12 * 2**20, transcendentals=0),
        name="grad_inputs",
    )(pos, a_own, a_par, b_own, b_par, weight, weight)


def grad_weight_kernel(pos, acts, a_own, a_par, b_own, b_par, out, lhs, turned):
    j = pl.program_id(0)
    half_steps = pl.num_programs(0) // 2

    def turn(half):
        for rel in range(2):
            core = pos[2] if rel == 0 else 1 - pos[2]
            for first in range(4):
                for second in range(4):
                    dx, dy = (second, first) if half == 0 else (first, second)
                    to = ((rel * 4 + first) * 4 + second) * 16
                    lhs[to : to + 16, :] = acts[rows_of(block_of(pos, dx, dy, core)), :]
        turned[...] = lhs[...].T

    def multiply(own, par):
        total = jnp.dot(turned[:, :256], own[...], preferred_element_type=F32)
        total += jnp.dot(turned[:, 256:], par[...], preferred_element_type=F32)
        out[...] = total.astype(BF)

    @pl.when(j == 0)
    def _():
        turn(0)

    @pl.when(j == half_steps)
    def _():
        turn(1)

    @pl.when(j < half_steps)
    def _():
        multiply(a_own, a_par)

    @pl.when(j >= half_steps)
    def _():
        multiply(b_own, b_par)


def grad_weight_of(pos, acts, a_own, a_par, b_own, b_par):
    width = 512
    early = pl.BlockSpec((256, width), lambda j, pos: (0, jnp.minimum(j, 5)))
    late = pl.BlockSpec((256, width), lambda j, pos: (0, jnp.maximum(j - 6, 0)))
    return pl.pallas_call(
        grad_weight_kernel,
        grid_spec=pltpu.PrefetchScalarGridSpec(
            num_scalar_prefetch=1,
            grid=(12,),
            in_specs=[pl.BlockSpec((512, 384), lambda j, pos: (0, 0)), early, early, late, late],
            out_specs=pl.BlockSpec((384, width), lambda j, pos: (0, j)),
            scratch_shapes=[pltpu.VMEM((512, 384), BF), pltpu.VMEM((384, 512), BF)],
        ),
        out_shape=jax.ShapeDtypeStruct((384, 6144), BF),
        compiler_params=pltpu.CompilerParams(vmem_limit_bytes=24 * 2**20),
        cost_estimate=pl.CostEstimate(flops=2 * 512 * 384 * 6144, bytes_accessed=12 * 2**20, transcendentals=0),
        name="grad_weight",
    )(pos, acts, a_own, a_par, b_own, b_par)


def body(inputs, weight, grad_out):
    core = lax.axis_index("core")
    pos = jnp.stack([lax.axis_index("x"), lax.axis_index("y"), core]).astype(jnp.int32)

    start_a, start_b = grad_out[:, :3072], grad_out[:, 3072:]
    a, b = {0: start_a}, {0: start_b}
    for d in STEPS:
        a[d] = get(start_a, "x", d)
        b[d] = get(start_b, "y", d)

    gathered = lax.all_to_all(jnp.broadcast_to(inputs[None], (8, 64, 384)), "z", 0, 0).reshape(512, 384)
    weight_par = swap(lax.dynamic_slice(weight, (0, (1 - core) * 3072), (384, 3072)))
    gathered_par = swap(gathered)

    row_a = jnp.concatenate([a[d] for d in range(4)])
    row_b = jnp.concatenate([b[d] for d in range(4)])
    a, b = {0: row_a}, {0: row_b}
    for d in STEPS:
        a[d] = get(row_a, "y", d)
        b[d] = get(row_b, "x", d)

    own_a, *send_a = project(0, pos, gathered, gathered_par, weight, weight_par)
    own_b, *send_b = project(1, pos, gathered, gathered_par, weight, weight_par)

    a_own = jnp.concatenate([a[d] for d in range(4)])
    b_own = jnp.concatenate([b[d] for d in range(4)])
    a_par, b_par = swap(a_own), swap(b_own)

    got_a = [get(v, "x", 4 - d) for v, d in zip(send_a, STEPS)]
    got_b = [get(v, "y", 4 - d) for v, d in zip(send_b, STEPS)]

    terms = grad_inputs_terms(pos, a_own, a_par, b_own, b_par, weight)
    grad_inputs = lax.all_to_all(terms.reshape(8, 64, 384), "z", 0, 0).sum(axis=0).astype(BF)
    grad_weight = grad_weight_of(pos, gathered, a_own, a_par, b_own, b_par)

    own_a, *send_a = relay(own_a, got_a)
    own_b, *send_b = relay(own_b, got_b)
    got_a = [get(v, "y", 4 - d) for v, d in zip(send_a, STEPS)]
    got_b = [get(v, "x", 4 - d) for v, d in zip(send_b, STEPS)]
    mine, theirs = finish(pos, own_a, *got_a, own_b, *got_b)
    other = swap(theirs)
    projected = jnp.where(
        core == 0, jnp.concatenate([mine, other], axis=1), jnp.concatenate([other, mine], axis=1)
    )
    return projected, grad_inputs, grad_weight


def solution(mesh):
    fine = Mesh(mesh.devices.reshape(4, 4, 2, 8), ("x", "y", "core", "z"))
    rows = ("x", "y", "core")
    placed = (P("z", rows), P(rows, "z"), P(rows, "z"))
    return jax.shard_map(
        body,
        mesh=fine,
        in_specs=placed,
        out_specs=(P(rows, "z"), P("z", rows), P(rows, "z")),
        check_vma=False,
    )
```

```python
import jax
import jax.numpy as jnp
from jax import lax
from jax.experimental import pallas as pl
from jax.experimental.pallas import tpu as pltpu
from jax.sharding import Mesh, PartitionSpec as P

BF = jnp.bfloat16
F32 = jnp.float32
SPAN = 124.5
LANES = 128
STEPS = (1, 3, 2)
ROWS = ("x", "y", "core")
VMEM = pl.BlockSpec(memory_space=pltpu.VMEM)
SMEM = pl.BlockSpec(memory_space=pltpu.SMEM)
HBM = pl.BlockSpec(memory_space=pltpu.HBM)


def index_of(x, y, core):
    return ((x % 4) * 4 + y % 4) * 2 + core


def ring(distance, second):
    pairs = []
    for x in range(4):
        for y in range(4):
            for core in range(2):
                dx, dy = (0, distance) if (core == 1) != second else (distance, 0)
                pairs.append((index_of(x + dx, y + dy, core), index_of(x, y, core)))
    return pairs


def get(value, distance, second):
    return lax.ppermute(value, ROWS, ring(distance, second))


def swap(value):
    return lax.ppermute(value, "core", [(0, 1), (1, 0)])


def encode(block):
    size = jnp.abs(block)
    top = jnp.maximum(jnp.max(size, axis=0, keepdims=True), 1e-30)
    top = (top * (1.0 + 2.0**-7)).astype(BF).astype(F32)
    level = jnp.exp2(size * (2 * SPAN / top) - SPAN)
    return jnp.where(block < 0, -level, level).astype(BF), top


def decode(code, top):
    code = code.astype(F32)
    size = (jnp.log2(jnp.abs(code)) + SPAN) * (top / (2 * SPAN))
    return jnp.where(code < 0, -size, size)


def block_at(pos, first, second, lead, core):
    dx = jnp.where(lead == 0, first, second)
    dy = jnp.where(lead == 0, second, first)
    return (((pos[0] + dx) % 4) * 4 + (pos[1] + dy) % 4) * 2 + core


def token_rows(block):
    return aligned(block * 16, 16)


def aligned(start, size):
    return pl.ds(pl.multiple_of(start, size), size)


def split_kernel(pos, weight, own, other, sems):
    copies = [
        pltpu.make_async_copy(weight.at[:, aligned(core * 3072, 3072)], out, sems.at[i])
        for i, (core, out) in enumerate(((1 - pos[2], other), (pos[2], own)))
    ]
    for copy in copies:
        copy.start()
    for copy in copies:
        copy.wait()


def split(pos, weight):
    return pl.pallas_call(
        split_kernel,
        in_specs=[SMEM, HBM],
        out_specs=[VMEM, VMEM],
        out_shape=[jax.ShapeDtypeStruct((384, 3072), BF)] * 2,
        scratch_shapes=[pltpu.SemaphoreType.DMA((2,))],
        compiler_params=pltpu.CompilerParams(vmem_limit_bytes=53 * 2**20),
        cost_estimate=pl.CostEstimate(flops=0, bytes_accessed=5 * 2**20, transcendentals=0),
        name="split",
    )(pos, weight)


def project_kernel(pos, own_in, par_in, w_own, w_par, out0, out1, out2, out3, lhs, tops, keep, sems):
    core = pos[2]
    tops[...] = jnp.zeros_like(tops)
    for first in range(4):
        for second in range(4):
            for to_core in range(2):
                to = ((first * 4 + second) * 2 + to_core) * 16
                rows = token_rows(block_at(pos, first, second, core, to_core))
                lhs[to : to + 16, :384] = own_in[rows, :]
                lhs[to : to + 16, 384:] = par_in[rows, :]

    def columns(j):
        rhs = jnp.concatenate([w_own[:, j * 512 : (j + 1) * 512], w_par[:, j * 512 : (j + 1) * 512]])
        total = jnp.dot(lhs[...], rhs, preferred_element_type=F32)
        for k in range(4):
            lanes = slice(k * LANES, (k + 1) * LANES)
            tile = j * 4 + k
            rows = slice(tile * 128, (tile + 1) * 128)
            keep[rows, :] = total[:128, lanes]
            for p, out in enumerate((out1, out2, out3)):
                d = STEPS[p]
                code, top = encode(total[d * 128 : (d + 1) * 128, lanes])
                out[rows, :] = code
                tops[p, tile : tile + 1, :] = top

    copies = []
    for j in range(6):
        columns(j)
        rows = slice(j * 512, (j + 1) * 512)
        copies.append(pltpu.make_async_copy(keep.at[rows, :], out0.at[rows, :], sems.at[j]))
        copies[j].start()
    for p, out in enumerate((out1, out2, out3)):
        out[3072:3104, :] = tops[p].astype(BF)
    for copy in copies:
        copy.wait()


def project(pos, own_in, par_in, weight, weight_par):
    piece = jax.ShapeDtypeStruct((3104, LANES), BF)
    return pl.pallas_call(
        project_kernel,
        in_specs=[SMEM, VMEM, VMEM, VMEM, VMEM],
        out_specs=[HBM] + [VMEM] * 3,
        out_shape=[jax.ShapeDtypeStruct((3072, LANES), F32), piece, piece, piece],
        scratch_shapes=[
            pltpu.VMEM((512, 768), BF),
            pltpu.VMEM((3, 32, LANES), F32),
            pltpu.VMEM((3072, LANES), F32),
            pltpu.SemaphoreType.DMA((6,)),
        ],
        compiler_params=pltpu.CompilerParams(vmem_limit_bytes=28 * 2**20),
        cost_estimate=pl.CostEstimate(flops=2 * 512 * 768 * 3072, bytes_accessed=10 * 2**20, transcendentals=2**20),
        name="project",
    )(pos, own_in, par_in, weight, weight_par)


def relay_kernel(own_in, in1, in2, in3, keep, out1, out2, out3, tops, own, sem):
    copy = pltpu.make_async_copy(own_in, own, sem)
    copy.start()
    tops[...] = jnp.zeros_like(tops)
    copy.wait()
    heads = [ref[3072:3104, :].astype(F32) for ref in (in1, in2, in3)]
    for j in range(24):
        rows = slice(j * 128, (j + 1) * 128)
        total = own[rows, :]
        for ref, head in zip((in1, in2, in3), heads):
            total += decode(ref[rows, :], head[j : j + 1, :])
        to = slice(j * 32, (j + 1) * 32)
        keep[to, :] = total[:32, :]
        for p, out in enumerate((out1, out2, out3)):
            d = STEPS[p]
            code, top = encode(total[d * 32 : (d + 1) * 32, :])
            out[to, :] = code
            tops[p, j : j + 1, :] = top
    for p, out in enumerate((out1, out2, out3)):
        out[768:800, :] = tops[p].astype(BF)


def relay(own, pieces):
    piece = jax.ShapeDtypeStruct((800, LANES), BF)
    return pl.pallas_call(
        relay_kernel,
        in_specs=[HBM] + [VMEM] * 3,
        out_specs=[VMEM] * 4,
        out_shape=[jax.ShapeDtypeStruct((768, LANES), F32), piece, piece, piece],
        scratch_shapes=[
            pltpu.VMEM((3, 32, LANES), F32),
            pltpu.VMEM((3072, LANES), F32),
            pltpu.SemaphoreType.DMA,
        ],
        compiler_params=pltpu.CompilerParams(vmem_limit_bytes=16 * 2**20),
        cost_estimate=pl.CostEstimate(flops=2**23, bytes_accessed=5 * 2**20, transcendentals=2**21),
        name="relay",
    )(own, *pieces)


def finish_kernel(pos, own, in1, in2, in3, keep, send):
    core = pos[2]
    heads = [ref[768:800, :].astype(F32) for ref in (in1, in2, in3)]
    for j in range(24):
        rows = slice(j * 32, (j + 1) * 32)
        total = own[rows, :]
        for ref, head in zip((in1, in2, in3), heads):
            total += decode(ref[rows, :], head[j : j + 1, :])
        lanes = slice(j * LANES, (j + 1) * LANES)
        low, high = total[:16, :].astype(BF), total[16:, :].astype(BF)
        keep[:, lanes] = jnp.where(core == 0, low, high)
        send[:, lanes] = jnp.where(core == 0, high, low)


def finish(pos, own, pieces):
    return pl.pallas_call(
        finish_kernel,
        in_specs=[SMEM] + [VMEM] * 4,
        out_specs=[VMEM] * 2,
        out_shape=[jax.ShapeDtypeStruct((16, 3072), BF)] * 2,
        compiler_params=pltpu.CompilerParams(vmem_limit_bytes=16 * 2**20),
        cost_estimate=pl.CostEstimate(flops=2**20, bytes_accessed=2**20, transcendentals=2**18),
        name="finish",
    )(pos, own, *pieces)


CONTRACT_LAST = (((1,), (1,)), ((), ()))


def places(pos):
    for rel in range(2):
        core = pos[2] if rel == 0 else 1 - pos[2]
        for second in range(4):
            for first in range(4):
                yield ((rel * 4 + second) * 4 + first) * 16, block_at(pos, first, second, core, core)


def grad_inputs_kernel(pos, *refs):
    pieces, (w_own, w_other, out, acc) = refs[:8], refs[8:]
    for weight, core in ((w_own, pos[2]), (w_other, 1 - pos[2])):
        cot = jnp.concatenate([ref[:, aligned(core * 3072, 3072)] for ref in pieces])
        term = lax.dot_general(cot, weight[...], CONTRACT_LAST, preferred_element_type=F32)
        acc[...] = term if weight is w_own else acc[...] + term
    for start, block in places(pos):
        out[token_rows(block), :] = acc[start : start + 16, :]


def grad_inputs_terms(pos, pieces, w_own, w_other):
    return pl.pallas_call(
        grad_inputs_kernel,
        in_specs=[SMEM] + [VMEM] * 10,
        out_specs=VMEM,
        out_shape=jax.ShapeDtypeStruct((512, 384), F32),
        scratch_shapes=[pltpu.VMEM((512, 384), F32)],
        compiler_params=pltpu.CompilerParams(vmem_limit_bytes=28 * 2**20),
        cost_estimate=pl.CostEstimate(flops=2 * 512 * 384 * 6144, bytes_accessed=12 * 2**20, transcendentals=0),
        name="grad_inputs",
    )(pos, *pieces, w_own, w_other)


def grad_weight_kernel(pos, acts, *refs):
    pieces, (out, lhs, slots, sems) = refs[:8], refs[8:]
    width = 1024
    for start, block in places(pos):
        lhs[start : start + 16, :] = acts[token_rows(block), :]
    copies = []
    for j in range(6):
        lanes = slice(j * width, (j + 1) * width)
        cot = jnp.concatenate([ref[:, lanes] for ref in pieces])
        slots[j] = lax.dot_general(
            lhs[...], cot, (((0,), (0,)), ((), ())), preferred_element_type=F32
        ).astype(BF)
        copies.append(pltpu.make_async_copy(slots.at[j], out.at[:, lanes], sems.at[j]))
        copies[j].start()
    for copy in copies:
        copy.wait()


def grad_weight_of(pos, acts, pieces):
    return pl.pallas_call(
        grad_weight_kernel,
        in_specs=[SMEM] + [VMEM] * 9,
        out_specs=HBM,
        out_shape=jax.ShapeDtypeStruct((384, 6144), BF),
        scratch_shapes=[
            pltpu.VMEM((512, 384), BF),
            pltpu.VMEM((6, 384, 1024), BF),
            pltpu.SemaphoreType.DMA((6,)),
        ],
        compiler_params=pltpu.CompilerParams(vmem_limit_bytes=28 * 2**20),
        cost_estimate=pl.CostEstimate(flops=2 * 512 * 384 * 6144, bytes_accessed=12 * 2**20, transcendentals=0),
        name="grad_weight",
    )(pos, acts, *pieces)


def body(inputs, weight, grad_out):
    core = lax.axis_index("core")
    pos = jnp.stack([lax.axis_index("x"), lax.axis_index("y"), core]).astype(jnp.int32)

    w_own, w_other = split(pos, weight)
    w_par = swap(w_other)
    grad_out, inputs, _ = lax.optimization_barrier((grad_out, inputs, w_other))

    blocks = {0: grad_out}
    for d in STEPS:
        blocks[d] = get(grad_out, d, False)

    line = jnp.concatenate([blocks[d] for d in range(4)])

    gathered = lax.all_to_all(jnp.broadcast_to(inputs[None], (8, 64, 384)), "z", 0, 0).reshape(512, 384)
    gathered_par = swap(gathered)

    pieces = {0: line}
    for d in STEPS:
        pieces[d] = get(line, d, True)

    own, *sends = project(pos, gathered, gathered_par, w_own, w_par)
    got = [get(v, 4 - d, False) for v, d in zip(sends, STEPS)]

    others = {0: swap(line)}
    late, _ = lax.optimization_barrier(({d: pieces[d] for d in STEPS}, own))
    for d in STEPS:
        pieces[d] = late[d]
        others[d] = swap(late[d])
    pieces = [pieces[d] for d in range(4)] + [others[d] for d in range(4)]
    terms = grad_inputs_terms(pos, pieces, w_own, w_other)
    grad_weight = grad_weight_of(pos, gathered, pieces)
    terms, grad_weight = lax.optimization_barrier((terms, grad_weight))
    grad_inputs = lax.all_to_all(terms.reshape(8, 64, 384), "z", 0, 0).sum(axis=0).astype(BF)

    own, *sends = relay(own, got)
    got = [get(v, 4 - d, True) for v, d in zip(sends, STEPS)]
    mine, theirs = finish(pos, own, got)
    other = swap(theirs)
    projected = jnp.where(
        core == 0, jnp.concatenate([mine, other], axis=1), jnp.concatenate([other, mine], axis=1)
    )
    return projected, grad_inputs, grad_weight


def solution(mesh):
    fine = Mesh(mesh.devices.reshape(4, 4, 2, 8), ("x", "y", "core", "z"))
    placed = (P("z", ROWS), P(ROWS, "z"), P(ROWS, "z"))
    return jax.shard_map(
        body,
        mesh=fine,
        in_specs=placed,
        out_specs=(P(ROWS, "z"), P("z", ROWS), P(ROWS, "z")),
        check_vma=False,
    )
```

```python
import jax
import jax.numpy as jnp
from jax import lax
from jax.experimental import pallas as pl
from jax.experimental.pallas import tpu as pltpu
from jax.sharding import Mesh, PartitionSpec as P

BF = jnp.bfloat16
F32 = jnp.float32
SPAN = 124.5
LANES = 128
STEPS = (1, 3, 2)
ROWS = ("x", "y", "core")
VMEM = pl.BlockSpec(memory_space=pltpu.VMEM)
SMEM = pl.BlockSpec(memory_space=pltpu.SMEM)
HBM = pl.BlockSpec(memory_space=pltpu.HBM)


def index_of(x, y, core):
    return ((x % 4) * 4 + y % 4) * 2 + core


def ring(distance, second):
    pairs = []
    for x in range(4):
        for y in range(4):
            for core in range(2):
                dx, dy = (0, distance) if (core == 1) != second else (distance, 0)
                pairs.append((index_of(x + dx, y + dy, core), index_of(x, y, core)))
    return pairs


def get(value, distance, second):
    return lax.ppermute(value, ROWS, ring(distance, second))


def swap(value):
    return lax.ppermute(value, "core", [(0, 1), (1, 0)])


def encode(block):
    size = jnp.abs(block)
    top = jnp.maximum(jnp.max(size, axis=0, keepdims=True), 1e-30)
    top = (top * (1.0 + 2.0**-7)).astype(BF).astype(F32)
    level = jnp.exp2(size * (2 * SPAN / top) - SPAN)
    return jnp.where(block < 0, -level, level).astype(BF), top


def decode(code, top):
    code = code.astype(F32)
    size = (jnp.log2(jnp.abs(code)) + SPAN) * (top / (2 * SPAN))
    return jnp.where(code < 0, -size, size)


def block_at(pos, first, second, lead, core):
    dx = jnp.where(lead == 0, first, second)
    dy = jnp.where(lead == 0, second, first)
    return (((pos[0] + dx) % 4) * 4 + (pos[1] + dy) % 4) * 2 + core


def token_rows(block):
    return aligned(block * 16, 16)


def aligned(start, size):
    return pl.ds(pl.multiple_of(start, size), size)


def project_kernel(
    pos, own_in, par_in, weight, w_par, out0, out1, out2, out3, lhs, rhs, tops, keep, codes, in_sems, out_sems, end_sems
):
    core = pos[2]
    reads, writes = [], []
    for j in range(12):
        lanes = slice(j * 512, (j + 1) * 512)
        reads.append(
            (
                pltpu.make_async_copy(weight.at[:, lanes], rhs.at[:384, lanes], in_sems.at[0, j]),
                pltpu.make_async_copy(w_par.at[:, lanes], rhs.at[384:, lanes], in_sems.at[1, j]),
            )
        )
        for read in reads[j]:
            read.start()
    tops[...] = jnp.zeros_like(tops)
    for first in range(4):
        for second in range(4):
            to = (first * 4 + second) * 16
            rows = token_rows(block_at(pos, first, second, core, core))
            lhs[to : to + 16, :384] = own_in[rows, :]
            lhs[to : to + 16, 384:] = par_in[rows, :]

    for j in range(12):
        for read in reads[j]:
            read.wait()
        total = jnp.dot(lhs[...], rhs[:, j * 512 : (j + 1) * 512], preferred_element_type=F32)
        for k in range(4):
            lanes = slice(k * LANES, (k + 1) * LANES)
            tile = j * 4 + k
            rows = slice(tile * 64, (tile + 1) * 64)
            keep[rows, :] = total[:64, lanes]
            for p in range(3):
                d = STEPS[p]
                code, top = encode(total[d * 64 : (d + 1) * 64, lanes])
                codes[p, rows, :] = code
                tops[p, tile : tile + 1, :] = top
        rows = slice(j * 256, (j + 1) * 256)
        writes.append(pltpu.make_async_copy(keep.at[rows, :], out0.at[rows, :], out_sems.at[0, j]))
        for p, out in enumerate((out1, out2, out3)):
            writes.append(pltpu.make_async_copy(codes.at[p, rows, :], out.at[rows, :], out_sems.at[p + 1, j]))
        for write in writes[-4:]:
            write.start()

    for p, out in enumerate((out1, out2, out3)):
        codes[p, 3072:3120, :] = tops[p].astype(BF)
        writes.append(pltpu.make_async_copy(codes.at[p, 3072:3120, :], out.at[3072:3120, :], end_sems.at[p]))
        writes[-1].start()
    for write in writes:
        write.wait()


def project(pos, own_in, par_in, weight, weight_par):
    piece = jax.ShapeDtypeStruct((3120, LANES), BF)
    return pl.pallas_call(
        project_kernel,
        in_specs=[SMEM, VMEM, VMEM, HBM, HBM],
        out_specs=[HBM] * 4,
        out_shape=[jax.ShapeDtypeStruct((3072, LANES), F32), piece, piece, piece],
        scratch_shapes=[
            pltpu.VMEM((256, 768), BF),
            pltpu.VMEM((768, 6144), BF),
            pltpu.VMEM((3, 48, LANES), F32),
            pltpu.VMEM((3072, LANES), F32),
            pltpu.VMEM((3, 3120, LANES), BF),
            pltpu.SemaphoreType.DMA((2, 12)),
            pltpu.SemaphoreType.DMA((4, 12)),
            pltpu.SemaphoreType.DMA((3,)),
        ],
        compiler_params=pltpu.CompilerParams(vmem_limit_bytes=56 * 2**20),
        cost_estimate=pl.CostEstimate(flops=2 * 512 * 768 * 3072, bytes_accessed=10 * 2**20, transcendentals=2**20),
        name="project",
    )(pos, own_in, par_in, weight, weight_par)


def relay_kernel(own_in, in1, in2, in3, keep, out1, out2, out3, tops, own, sem):
    copy = pltpu.make_async_copy(own_in, own, sem)
    copy.start()
    tops[...] = jnp.zeros_like(tops)
    copy.wait()
    heads = [ref[3072:3120, :].astype(F32) for ref in (in1, in2, in3)]
    for j in range(48):
        rows = slice(j * 64, (j + 1) * 64)
        total = own[rows, :]
        for ref, head in zip((in1, in2, in3), heads):
            total += decode(ref[rows, :], head[j : j + 1, :])
        to = slice(j * 16, (j + 1) * 16)
        keep[to, :] = total[:16, :]
        for p, out in enumerate((out1, out2, out3)):
            d = STEPS[p]
            code, top = encode(total[d * 16 : (d + 1) * 16, :])
            out[to, :] = code
            tops[p, j : j + 1, :] = top
    for p, out in enumerate((out1, out2, out3)):
        out[768:816, :] = tops[p].astype(BF)


def relay(own, pieces):
    piece = jax.ShapeDtypeStruct((816, LANES), BF)
    return pl.pallas_call(
        relay_kernel,
        in_specs=[HBM] + [VMEM] * 3,
        out_specs=[VMEM] * 4,
        out_shape=[jax.ShapeDtypeStruct((768, LANES), F32), piece, piece, piece],
        scratch_shapes=[
            pltpu.VMEM((3, 48, LANES), F32),
            pltpu.VMEM((3072, LANES), F32),
            pltpu.SemaphoreType.DMA,
        ],
        compiler_params=pltpu.CompilerParams(vmem_limit_bytes=16 * 2**20),
        cost_estimate=pl.CostEstimate(flops=2**23, bytes_accessed=5 * 2**20, transcendentals=2**21),
        name="relay",
    )(own, *pieces)


def finish_kernel(own, in1, in2, in3, out):
    heads = [ref[768:816, :].astype(F32) for ref in (in1, in2, in3)]
    for j in range(48):
        rows = slice(j * 16, (j + 1) * 16)
        total = own[rows, :]
        for ref, head in zip((in1, in2, in3), heads):
            total += decode(ref[rows, :], head[j : j + 1, :])
        out[:, j * LANES : (j + 1) * LANES] = total.astype(BF)


def finish(own, pieces):
    return pl.pallas_call(
        finish_kernel,
        in_specs=[VMEM] * 4,
        out_specs=VMEM,
        out_shape=jax.ShapeDtypeStruct((16, 6144), BF),
        compiler_params=pltpu.CompilerParams(vmem_limit_bytes=16 * 2**20),
        cost_estimate=pl.CostEstimate(flops=2**33, bytes_accessed=2**20, transcendentals=2**18),
        name="finish",
    )(own, *pieces)


CONTRACT_LAST = (((1,), (1,)), ((), ()))


def places(pos):
    for rel in range(2):
        core = pos[2] if rel == 0 else 1 - pos[2]
        for second in range(4):
            for first in range(4):
                yield ((rel * 4 + second) * 4 + first) * 16, block_at(pos, first, second, core, core)


def grad_inputs_kernel(pos, *refs):
    pieces, (weight, out, acc) = refs[:8], refs[8:]
    for half in range(2):
        lanes = slice(half * 3072, (half + 1) * 3072)
        cot = jnp.concatenate([ref[:, lanes] for ref in pieces])
        term = lax.dot_general(cot, weight[:, lanes], CONTRACT_LAST, preferred_element_type=F32)
        acc[...] = term if half == 0 else acc[...] + term
    for start, block in places(pos):
        out[token_rows(block), :] = acc[start : start + 16, :]


def grad_inputs_terms(pos, pieces, weight):
    return pl.pallas_call(
        grad_inputs_kernel,
        in_specs=[SMEM] + [VMEM] * 9,
        out_specs=VMEM,
        out_shape=jax.ShapeDtypeStruct((512, 384), F32),
        scratch_shapes=[pltpu.VMEM((512, 384), F32)],
        compiler_params=pltpu.CompilerParams(vmem_limit_bytes=28 * 2**20),
        cost_estimate=pl.CostEstimate(flops=2 * 512 * 384 * 6144, bytes_accessed=12 * 2**20, transcendentals=0),
        name="grad_inputs",
    )(pos, *pieces, weight)


def grad_weight_kernel(pos, acts, *refs):
    pieces, (out, lhs, slots, sems) = refs[:8], refs[8:]
    width = 1024
    for start, block in places(pos):
        lhs[start : start + 16, :] = acts[token_rows(block), :]
    copies = []
    for j in range(6):
        lanes = slice(j * width, (j + 1) * width)
        cot = jnp.concatenate([ref[:, lanes] for ref in pieces])
        slots[j] = lax.dot_general(
            lhs[...], cot, (((0,), (0,)), ((), ())), preferred_element_type=F32
        ).astype(BF)
        copies.append(pltpu.make_async_copy(slots.at[j], out.at[:, lanes], sems.at[j]))
        copies[j].start()
    for copy in copies:
        copy.wait()


def grad_weight_of(pos, acts, pieces):
    return pl.pallas_call(
        grad_weight_kernel,
        in_specs=[SMEM] + [VMEM] * 9,
        out_specs=HBM,
        out_shape=jax.ShapeDtypeStruct((384, 6144), BF),
        scratch_shapes=[
            pltpu.VMEM((512, 384), BF),
            pltpu.VMEM((6, 384, 1024), BF),
            pltpu.SemaphoreType.DMA((6,)),
        ],
        compiler_params=pltpu.CompilerParams(vmem_limit_bytes=28 * 2**20),
        cost_estimate=pl.CostEstimate(flops=2 * 512 * 384 * 6144, bytes_accessed=12 * 2**20, transcendentals=0),
        name="grad_weight",
    )(pos, acts, *pieces)


def body(inputs, weight, grad_out):
    core = lax.axis_index("core")
    pos = jnp.stack([lax.axis_index("x"), lax.axis_index("y"), core]).astype(jnp.int32)

    w_par = swap(weight)

    blocks = {0: grad_out}
    for d in STEPS:
        blocks[d] = get(grad_out, d, False)

    line = jnp.concatenate([blocks[d] for d in range(4)])

    gathered = lax.all_to_all(jnp.broadcast_to(inputs[None], (8, 64, 384)), "z", 0, 0).reshape(512, 384)
    gathered_par = swap(gathered)

    pieces = {0: line}
    for d in STEPS:
        pieces[d] = get(line, d, True)

    own, *sends = project(pos, gathered, gathered_par, weight, w_par)
    got = [get(v, 4 - d, False) for v, d in zip(sends, STEPS)]

    others = {0: swap(line)}
    late, _ = lax.optimization_barrier(({d: pieces[d] for d in STEPS}, own))
    for d in STEPS:
        pieces[d] = late[d]
        others[d] = swap(late[d])
    pieces = [pieces[d] for d in range(4)] + [others[d] for d in range(4)]
    terms = grad_inputs_terms(pos, pieces, weight)
    grad_weight = grad_weight_of(pos, gathered, pieces)
    terms, grad_weight = lax.optimization_barrier((terms, grad_weight))
    grad_inputs = lax.all_to_all(terms.reshape(8, 64, 384), "z", 0, 0).sum(axis=0).astype(BF)

    own, grad_weight = lax.optimization_barrier((own, grad_weight))
    own, *sends = relay(own, got)
    got = [get(v, 4 - d, True) for v, d in zip(sends, STEPS)]
    return finish(own, got), grad_inputs, grad_weight


def solution(mesh):
    fine = Mesh(mesh.devices.reshape(4, 4, 2, 8), ("x", "y", "core", "z"))
    placed = (P("z", ROWS), P(ROWS, "z"), P(ROWS, "z"))
    return jax.shard_map(
        body,
        mesh=fine,
        in_specs=placed,
        out_specs=(P(ROWS, "z"), P("z", ROWS), P(ROWS, "z")),
        check_vma=False,
    )
```

```python
import jax
import jax.numpy as jnp
from jax import lax
from jax.experimental import pallas as pl
from jax.experimental.pallas import tpu as pltpu
from jax.sharding import Mesh, PartitionSpec as P

BF = jnp.bfloat16
F32 = jnp.float32
SPAN = 124.5
LANES = 128
STEPS = (1, 3, 2)
ROWS = ("x", "y", "core")
VMEM = pl.BlockSpec(memory_space=pltpu.VMEM)
SMEM = pl.BlockSpec(memory_space=pltpu.SMEM)
HBM = pl.BlockSpec(memory_space=pltpu.HBM)


def index_of(x, y, core):
    return ((x % 4) * 4 + y % 4) * 2 + core


def ring(distance, second):
    pairs = []
    for x in range(4):
        for y in range(4):
            for core in range(2):
                dx, dy = (0, distance) if (core == 1) != second else (distance, 0)
                pairs.append((index_of(x + dx, y + dy, core), index_of(x, y, core)))
    return pairs


def get(value, distance, second):
    return lax.ppermute(value, ROWS, ring(distance, second))


def swap(value):
    return lax.ppermute(value, "core", [(0, 1), (1, 0)])


def encode(block):
    size = jnp.abs(block)
    top = jnp.maximum(jnp.max(size, axis=0, keepdims=True), 1e-30)
    top = (top * (1.0 + 2.0**-7)).astype(BF).astype(F32)
    level = jnp.exp2(size * (2 * SPAN / top) - SPAN)
    return jnp.where(block < 0, -level, level).astype(BF), top


def decode(code, top):
    code = code.astype(F32)
    size = (jnp.log2(jnp.abs(code)) + SPAN) * (top / (2 * SPAN))
    return jnp.where(code < 0, -size, size)


def block_at(pos, first, second, lead, core):
    dx = jnp.where(lead == 0, first, second)
    dy = jnp.where(lead == 0, second, first)
    return (((pos[0] + dx) % 4) * 4 + (pos[1] + dy) % 4) * 2 + core


def token_rows(block):
    return aligned(block * 16, 16)


def aligned(start, size):
    return pl.ds(pl.multiple_of(start, size), size)


def project_kernel(
    pos, own_in, par_in, weight, w_par, out0, out1, out2, out3, lhs, rhs, tops, keep, codes, in_sems, out_sems, end_sems
):
    core = pos[2]
    reads, writes = [], []
    for j in range(12):
        lanes = slice(j * 512, (j + 1) * 512)
        reads.append(
            (
                pltpu.make_async_copy(weight.at[:, lanes], rhs.at[:384, lanes], in_sems.at[0, j]),
                pltpu.make_async_copy(w_par.at[:, lanes], rhs.at[384:, lanes], in_sems.at[1, j]),
            )
        )
        for read in reads[j]:
            read.start()
    tops[...] = jnp.zeros_like(tops)
    for first in range(4):
        for second in range(4):
            to = (first * 4 + second) * 16
            rows = token_rows(block_at(pos, first, second, core, core))
            lhs[to : to + 16, :384] = own_in[rows, :]
            lhs[to : to + 16, 384:] = par_in[rows, :]

    for j in range(12):
        for read in reads[j]:
            read.wait()
        total = jnp.dot(lhs[...], rhs[:, j * 512 : (j + 1) * 512], preferred_element_type=F32)
        for k in range(4):
            lanes = slice(k * LANES, (k + 1) * LANES)
            tile = j * 4 + k
            rows = slice(tile * 64, (tile + 1) * 64)
            keep[rows, :] = total[:64, lanes]
            for p in range(3):
                d = STEPS[p]
                code, top = encode(total[d * 64 : (d + 1) * 64, lanes])
                codes[p, rows, :] = code
                tops[p, tile : tile + 1, :] = top
        rows = slice(j * 256, (j + 1) * 256)
        writes.append(pltpu.make_async_copy(keep.at[rows, :], out0.at[rows, :], out_sems.at[0, j]))
        for p, out in enumerate((out1, out2, out3)):
            writes.append(pltpu.make_async_copy(codes.at[p, rows, :], out.at[rows, :], out_sems.at[p + 1, j]))
        for write in writes[-4:]:
            write.start()

    for p, out in enumerate((out1, out2, out3)):
        codes[p, 3072:3120, :] = tops[p].astype(BF)
        writes.append(pltpu.make_async_copy(codes.at[p, 3072:3120, :], out.at[3072:3120, :], end_sems.at[p]))
        writes[-1].start()
    for write in writes:
        write.wait()


def project(pos, own_in, par_in, weight, weight_par):
    piece = jax.ShapeDtypeStruct((3120, LANES), BF)
    return pl.pallas_call(
        project_kernel,
        in_specs=[SMEM, VMEM, VMEM, HBM, HBM],
        out_specs=[HBM] * 4,
        out_shape=[jax.ShapeDtypeStruct((3072, LANES), F32), piece, piece, piece],
        scratch_shapes=[
            pltpu.VMEM((256, 768), BF),
            pltpu.VMEM((768, 6144), BF),
            pltpu.VMEM((3, 48, LANES), F32),
            pltpu.VMEM((3072, LANES), F32),
            pltpu.VMEM((3, 3120, LANES), BF),
            pltpu.SemaphoreType.DMA((2, 12)),
            pltpu.SemaphoreType.DMA((4, 12)),
            pltpu.SemaphoreType.DMA((3,)),
        ],
        compiler_params=pltpu.CompilerParams(vmem_limit_bytes=56 * 2**20),
        cost_estimate=pl.CostEstimate(flops=2 * 512 * 768 * 3072, bytes_accessed=10 * 2**20, transcendentals=2**20),
        name="project",
    )(pos, own_in, par_in, weight, weight_par)


def relay_kernel(own_in, in1, in2, in3, keep, out1, out2, out3, tops, own, sem):
    copy = pltpu.make_async_copy(own_in, own, sem)
    copy.start()
    tops[...] = jnp.zeros_like(tops)
    copy.wait()
    heads = [ref[3072:3120, :].astype(F32) for ref in (in1, in2, in3)]
    for j in range(48):
        rows = slice(j * 64, (j + 1) * 64)
        total = own[rows, :]
        for ref, head in zip((in1, in2, in3), heads):
            total += decode(ref[rows, :], head[j : j + 1, :])
        to = slice(j * 16, (j + 1) * 16)
        keep[to, :] = total[:16, :]
        for p, out in enumerate((out1, out2, out3)):
            d = STEPS[p]
            code, top = encode(total[d * 16 : (d + 1) * 16, :])
            out[to, :] = code
            tops[p, j : j + 1, :] = top
    for p, out in enumerate((out1, out2, out3)):
        out[768:816, :] = tops[p].astype(BF)


def relay(own, pieces):
    piece = jax.ShapeDtypeStruct((816, LANES), BF)
    return pl.pallas_call(
        relay_kernel,
        in_specs=[HBM] + [VMEM] * 3,
        out_specs=[VMEM] * 4,
        out_shape=[jax.ShapeDtypeStruct((768, LANES), F32), piece, piece, piece],
        scratch_shapes=[
            pltpu.VMEM((3, 48, LANES), F32),
            pltpu.VMEM((3072, LANES), F32),
            pltpu.SemaphoreType.DMA,
        ],
        compiler_params=pltpu.CompilerParams(vmem_limit_bytes=16 * 2**20),
        cost_estimate=pl.CostEstimate(flops=2**23, bytes_accessed=5 * 2**20, transcendentals=2**21),
        name="relay",
    )(own, *pieces)


def finish_kernel(own, in1, in2, in3, out):
    heads = [ref[768:816, :].astype(F32) for ref in (in1, in2, in3)]
    for j in range(48):
        rows = slice(j * 16, (j + 1) * 16)
        total = own[rows, :]
        for ref, head in zip((in1, in2, in3), heads):
            total += decode(ref[rows, :], head[j : j + 1, :])
        out[:, j * LANES : (j + 1) * LANES] = total.astype(BF)


def finish(own, pieces):
    return pl.pallas_call(
        finish_kernel,
        in_specs=[VMEM] * 4,
        out_specs=VMEM,
        out_shape=jax.ShapeDtypeStruct((16, 6144), BF),
        compiler_params=pltpu.CompilerParams(vmem_limit_bytes=16 * 2**20),
        cost_estimate=pl.CostEstimate(flops=2**32, bytes_accessed=2**20, transcendentals=2**18),
        name="finish",
    )(own, *pieces)


CONTRACT_LAST = (((1,), (1,)), ((), ()))


def places(pos):
    for rel in range(2):
        core = pos[2] if rel == 0 else 1 - pos[2]
        for second in range(4):
            for first in range(4):
                yield ((rel * 4 + second) * 4 + first) * 16, block_at(pos, first, second, core, core)


def grad_inputs_kernel(pos, *refs):
    pieces, (weight, out, acc) = refs[:8], refs[8:]
    for half in range(2):
        lanes = slice(half * 3072, (half + 1) * 3072)
        cot = jnp.concatenate([ref[:, lanes] for ref in pieces])
        term = lax.dot_general(cot, weight[:, lanes], CONTRACT_LAST, preferred_element_type=F32)
        acc[...] = term if half == 0 else acc[...] + term
    for start, block in places(pos):
        out[token_rows(block), :] = acc[start : start + 16, :]


def grad_inputs_terms(pos, pieces, weight):
    return pl.pallas_call(
        grad_inputs_kernel,
        in_specs=[SMEM] + [VMEM] * 9,
        out_specs=VMEM,
        out_shape=jax.ShapeDtypeStruct((512, 384), F32),
        scratch_shapes=[pltpu.VMEM((512, 384), F32)],
        compiler_params=pltpu.CompilerParams(vmem_limit_bytes=28 * 2**20),
        cost_estimate=pl.CostEstimate(flops=2 * 512 * 384 * 6144, bytes_accessed=12 * 2**20, transcendentals=0),
        name="grad_inputs",
    )(pos, *pieces, weight)


def grad_weight_kernel(pos, acts, *refs):
    pieces, (out, lhs, slots, sems) = refs[:8], refs[8:]
    width = 1024
    for start, block in places(pos):
        lhs[start : start + 16, :] = acts[token_rows(block), :]
    copies = []
    for j in range(6):
        lanes = slice(j * width, (j + 1) * width)
        cot = jnp.concatenate([ref[:, lanes] for ref in pieces])
        slots[j] = lax.dot_general(
            lhs[...], cot, (((0,), (0,)), ((), ())), preferred_element_type=F32
        ).astype(BF)
        copies.append(pltpu.make_async_copy(slots.at[j], out.at[:, lanes], sems.at[j]))
        copies[j].start()
    for copy in copies:
        copy.wait()


def grad_weight_of(pos, acts, pieces):
    return pl.pallas_call(
        grad_weight_kernel,
        in_specs=[SMEM] + [VMEM] * 9,
        out_specs=HBM,
        out_shape=jax.ShapeDtypeStruct((384, 6144), BF),
        scratch_shapes=[
            pltpu.VMEM((512, 384), BF),
            pltpu.VMEM((6, 384, 1024), BF),
            pltpu.SemaphoreType.DMA((6,)),
        ],
        compiler_params=pltpu.CompilerParams(vmem_limit_bytes=28 * 2**20),
        cost_estimate=pl.CostEstimate(flops=2 * 512 * 384 * 6144, bytes_accessed=12 * 2**20, transcendentals=0),
        name="grad_weight",
    )(pos, acts, *pieces)


def body(inputs, weight, grad_out):
    core = lax.axis_index("core")
    pos = jnp.stack([lax.axis_index("x"), lax.axis_index("y"), core]).astype(jnp.int32)

    w_par = swap(weight)

    blocks = {0: grad_out}
    for d in STEPS:
        blocks[d] = get(grad_out, d, False)

    line = jnp.concatenate([blocks[d] for d in range(4)])

    gathered = lax.all_to_all(jnp.broadcast_to(inputs[None], (8, 64, 384)), "z", 0, 0).reshape(512, 384)
    gathered_par = swap(gathered)

    pieces = {0: line}
    for d in STEPS:
        pieces[d] = get(line, d, True)

    own, *sends = project(pos, gathered, gathered_par, weight, w_par)
    got = [get(v, 4 - d, False) for v, d in zip(sends, STEPS)]

    others = {0: swap(line)}
    late, _ = lax.optimization_barrier(({d: pieces[d] for d in STEPS}, own))
    for d in STEPS:
        pieces[d] = late[d]
        others[d] = swap(late[d])
    pieces = [pieces[d] for d in range(4)] + [others[d] for d in range(4)]
    terms = grad_inputs_terms(pos, pieces, weight)
    grad_inputs = lax.all_to_all(terms.reshape(8, 64, 384), "z", 0, 0).sum(axis=0).astype(BF)

    own, *sends = relay(own, got)
    pieces, own = lax.optimization_barrier((pieces, own))
    grad_weight = grad_weight_of(pos, gathered, pieces)
    got = [get(v, 4 - d, True) for v, d in zip(sends, STEPS)]
    return finish(own, got), grad_inputs, grad_weight


def solution(mesh):
    fine = Mesh(mesh.devices.reshape(4, 4, 2, 8), ("x", "y", "core", "z"))
    placed = (P("z", ROWS), P(ROWS, "z"), P(ROWS, "z"))
    return jax.shard_map(
        body,
        mesh=fine,
        in_specs=placed,
        out_specs=(P(ROWS, "z"), P("z", ROWS), P(ROWS, "z")),
        check_vma=False,
    )
```

```python
import jax
import jax.numpy as jnp
from jax import lax
from jax.experimental import pallas as pl
from jax.experimental.pallas import tpu as pltpu
from jax.sharding import Mesh, PartitionSpec as P

BF = jnp.bfloat16
F32 = jnp.float32
SPAN = 124.5
LANES = 128
STEPS = (1, 3, 2)
ROWS = ("x", "y", "core")
VMEM = pl.BlockSpec(memory_space=pltpu.VMEM)
SMEM = pl.BlockSpec(memory_space=pltpu.SMEM)
HBM = pl.BlockSpec(memory_space=pltpu.HBM)


def index_of(x, y, core):
    return ((x % 4) * 4 + y % 4) * 2 + core


def ring(distance, second):
    pairs = []
    for x in range(4):
        for y in range(4):
            for core in range(2):
                dx, dy = (0, distance) if (core == 1) != second else (distance, 0)
                pairs.append((index_of(x + dx, y + dy, core), index_of(x, y, core)))
    return pairs


def get(value, distance, second):
    return lax.ppermute(value, ROWS, ring(distance, second))


def swap(value):
    return lax.ppermute(value, "core", [(0, 1), (1, 0)])


def encode(block):
    size = jnp.abs(block)
    top = jnp.maximum(jnp.max(size, axis=0, keepdims=True), 1e-30)
    top = (top * (1.0 + 2.0**-7)).astype(BF).astype(F32)
    level = jnp.exp2(size * (2 * SPAN / top) - SPAN)
    return jnp.where(block < 0, -level, level).astype(BF), top


def decode(code, top):
    code = code.astype(F32)
    size = (jnp.log2(jnp.abs(code)) + SPAN) * (top / (2 * SPAN))
    return jnp.where(code < 0, -size, size)


def block_at(pos, first, second, lead, core):
    dx = jnp.where(lead == 0, first, second)
    dy = jnp.where(lead == 0, second, first)
    return (((pos[0] + dx) % 4) * 4 + (pos[1] + dy) % 4) * 2 + core


def token_rows(block):
    return aligned(block * 16, 16)


def aligned(start, size):
    return pl.ds(pl.multiple_of(start, size), size)


def project_kernel(
    pos, own_in, par_in, weight, w_par, out0, out1, out2, out3, lhs, rhs, tops, keep, codes, in_sems, out_sems, end_sems
):
    core = pos[2]
    reads, writes = [], []
    for j in range(12):
        lanes = slice(j * 512, (j + 1) * 512)
        reads.append(
            (
                pltpu.make_async_copy(weight.at[:, lanes], rhs.at[:384, lanes], in_sems.at[0, j]),
                pltpu.make_async_copy(w_par.at[:, lanes], rhs.at[384:, lanes], in_sems.at[1, j]),
            )
        )
        for read in reads[j]:
            read.start()
    tops[...] = jnp.zeros_like(tops)
    for first in range(4):
        for second in range(4):
            to = (first * 4 + second) * 16
            rows = token_rows(block_at(pos, first, second, core, core))
            lhs[to : to + 16, :384] = own_in[rows, :]
            lhs[to : to + 16, 384:] = par_in[rows, :]

    for j in range(12):
        for read in reads[j]:
            read.wait()
        total = jnp.dot(lhs[...], rhs[:, j * 512 : (j + 1) * 512], preferred_element_type=F32)
        for k in range(4):
            lanes = slice(k * LANES, (k + 1) * LANES)
            tile = j * 4 + k
            rows = slice(tile * 64, (tile + 1) * 64)
            keep[rows, :] = total[:64, lanes]
            for p in range(3):
                d = STEPS[p]
                code, top = encode(total[d * 64 : (d + 1) * 64, lanes])
                codes[p, rows, :] = code
                tops[p, tile : tile + 1, :] = top
        rows = slice(j * 256, (j + 1) * 256)
        writes.append(pltpu.make_async_copy(keep.at[rows, :], out0.at[rows, :], out_sems.at[0, j]))
        for p, out in enumerate((out1, out2, out3)):
            writes.append(pltpu.make_async_copy(codes.at[p, rows, :], out.at[rows, :], out_sems.at[p + 1, j]))
        for write in writes[-4:]:
            write.start()

    for p, out in enumerate((out1, out2, out3)):
        codes[p, 3072:3120, :] = tops[p].astype(BF)
        writes.append(pltpu.make_async_copy(codes.at[p, 3072:3120, :], out.at[3072:3120, :], end_sems.at[p]))
        writes[-1].start()
    for write in writes:
        write.wait()


def project(pos, own_in, par_in, weight, weight_par):
    piece = jax.ShapeDtypeStruct((3120, LANES), BF)
    return pl.pallas_call(
        project_kernel,
        in_specs=[SMEM, VMEM, VMEM, HBM, HBM],
        out_specs=[HBM] * 4,
        out_shape=[jax.ShapeDtypeStruct((3072, LANES), F32), piece, piece, piece],
        scratch_shapes=[
            pltpu.VMEM((256, 768), BF),
            pltpu.VMEM((768, 6144), BF),
            pltpu.VMEM((3, 48, LANES), F32),
            pltpu.VMEM((3072, LANES), F32),
            pltpu.VMEM((3, 3120, LANES), BF),
            pltpu.SemaphoreType.DMA((2, 12)),
            pltpu.SemaphoreType.DMA((4, 12)),
            pltpu.SemaphoreType.DMA((3,)),
        ],
        compiler_params=pltpu.CompilerParams(vmem_limit_bytes=56 * 2**20),
        cost_estimate=pl.CostEstimate(flops=2 * 512 * 768 * 3072, bytes_accessed=10 * 2**20, transcendentals=2**20),
        name="project",
    )(pos, own_in, par_in, weight, weight_par)


def relay_kernel(own_in, in1, in2, in3, keep, out1, out2, out3, tops, own, sem):
    copy = pltpu.make_async_copy(own_in, own, sem)
    copy.start()
    tops[...] = jnp.zeros_like(tops)
    copy.wait()
    heads = [ref[3072:3120, :].astype(F32) for ref in (in1, in2, in3)]
    for j in range(48):
        rows = slice(j * 64, (j + 1) * 64)
        total = own[rows, :]
        for ref, head in zip((in1, in2, in3), heads):
            total += decode(ref[rows, :], head[j : j + 1, :])
        to = slice(j * 16, (j + 1) * 16)
        keep[to, :] = total[:16, :]
        for p, out in enumerate((out1, out2, out3)):
            d = STEPS[p]
            code, top = encode(total[d * 16 : (d + 1) * 16, :])
            out[to, :] = code
            tops[p, j : j + 1, :] = top
    for p, out in enumerate((out1, out2, out3)):
        out[768:816, :] = tops[p].astype(BF)


def relay(own, pieces):
    piece = jax.ShapeDtypeStruct((816, LANES), BF)
    return pl.pallas_call(
        relay_kernel,
        in_specs=[HBM] + [VMEM] * 3,
        out_specs=[VMEM] * 4,
        out_shape=[jax.ShapeDtypeStruct((768, LANES), F32), piece, piece, piece],
        scratch_shapes=[
            pltpu.VMEM((3, 48, LANES), F32),
            pltpu.VMEM((3072, LANES), F32),
            pltpu.SemaphoreType.DMA,
        ],
        compiler_params=pltpu.CompilerParams(vmem_limit_bytes=16 * 2**20),
        cost_estimate=pl.CostEstimate(flops=2**23, bytes_accessed=5 * 2**20, transcendentals=2**21),
        name="relay",
    )(own, *pieces)


def finish_kernel(own, in1, in2, in3, out):
    heads = [ref[768:816, :].astype(F32) for ref in (in1, in2, in3)]
    for j in range(48):
        rows = slice(j * 16, (j + 1) * 16)
        total = own[rows, :]
        for ref, head in zip((in1, in2, in3), heads):
            total += decode(ref[rows, :], head[j : j + 1, :])
        out[:, j * LANES : (j + 1) * LANES] = total.astype(BF)


def finish(own, pieces):
    return pl.pallas_call(
        finish_kernel,
        in_specs=[VMEM] * 4,
        out_specs=VMEM,
        out_shape=jax.ShapeDtypeStruct((16, 6144), BF),
        compiler_params=pltpu.CompilerParams(vmem_limit_bytes=16 * 2**20),
        cost_estimate=pl.CostEstimate(flops=2**32, bytes_accessed=2**20, transcendentals=2**18),
        name="finish",
    )(own, *pieces)


CONTRACT_LAST = (((1,), (1,)), ((), ()))


def places(pos):
    for rel in range(2):
        core = pos[2] if rel == 0 else 1 - pos[2]
        for second in range(4):
            for first in range(4):
                yield ((rel * 4 + second) * 4 + first) * 16, block_at(pos, first, second, core, core)


def grad_inputs_kernel(pos, *refs):
    pieces, (weight, out, acc) = refs[:8], refs[8:]
    for half in range(2):
        lanes = slice(half * 3072, (half + 1) * 3072)
        cot = jnp.concatenate([ref[:, lanes] for ref in pieces])
        term = lax.dot_general(cot, weight[:, lanes], CONTRACT_LAST, preferred_element_type=F32)
        acc[...] = term if half == 0 else acc[...] + term
    for start, block in places(pos):
        out[token_rows(block), :] = acc[start : start + 16, :]


def grad_inputs_terms(pos, pieces, weight):
    return pl.pallas_call(
        grad_inputs_kernel,
        in_specs=[SMEM] + [VMEM] * 9,
        out_specs=VMEM,
        out_shape=jax.ShapeDtypeStruct((512, 384), F32),
        scratch_shapes=[pltpu.VMEM((512, 384), F32)],
        compiler_params=pltpu.CompilerParams(vmem_limit_bytes=28 * 2**20),
        cost_estimate=pl.CostEstimate(flops=2 * 512 * 384 * 6144, bytes_accessed=12 * 2**20, transcendentals=0),
        name="grad_inputs",
    )(pos, *pieces, weight)


def grad_weight_kernel(pos, acts, *refs):
    pieces, (out, lhs, slots, sems) = refs[:8], refs[8:]
    width = 1024
    for start, block in places(pos):
        lhs[start : start + 16, :] = acts[token_rows(block), :]
    copies = []
    for j in range(6):
        lanes = slice(j * width, (j + 1) * width)
        cot = jnp.concatenate([ref[:, lanes] for ref in pieces])
        slots[j] = lax.dot_general(
            lhs[...], cot, (((0,), (0,)), ((), ())), preferred_element_type=F32
        ).astype(BF)
        copies.append(pltpu.make_async_copy(slots.at[j], out.at[:, lanes], sems.at[j]))
        copies[j].start()
    for copy in copies:
        copy.wait()


def grad_weight_of(pos, acts, pieces):
    return pl.pallas_call(
        grad_weight_kernel,
        in_specs=[SMEM] + [VMEM] * 9,
        out_specs=HBM,
        out_shape=jax.ShapeDtypeStruct((384, 6144), BF),
        scratch_shapes=[
            pltpu.VMEM((512, 384), BF),
            pltpu.VMEM((6, 384, 1024), BF),
            pltpu.SemaphoreType.DMA((6,)),
        ],
        compiler_params=pltpu.CompilerParams(vmem_limit_bytes=58 * 2**20),
        cost_estimate=pl.CostEstimate(flops=2 * 512 * 384 * 6144, bytes_accessed=12 * 2**20, transcendentals=0),
        name="grad_weight",
    )(pos, acts, *pieces)


def body(inputs, weight, grad_out):
    core = lax.axis_index("core")
    pos = jnp.stack([lax.axis_index("x"), lax.axis_index("y"), core]).astype(jnp.int32)

    w_par = swap(weight)

    blocks = {0: grad_out}
    for d in STEPS:
        blocks[d] = get(grad_out, d, False)

    line = jnp.concatenate([blocks[d] for d in range(4)])

    gathered = lax.all_to_all(jnp.broadcast_to(inputs[None], (8, 64, 384)), "z", 0, 0).reshape(512, 384)
    gathered_par = swap(gathered)

    pieces = {0: line}
    for d in STEPS:
        pieces[d] = get(line, d, True)

    own, *sends = project(pos, gathered, gathered_par, weight, w_par)
    got = [get(v, 4 - d, False) for v, d in zip(sends, STEPS)]

    others = {0: swap(line)}
    late, _ = lax.optimization_barrier(({d: pieces[d] for d in STEPS}, own))
    for d in STEPS:
        pieces[d] = late[d]
        others[d] = swap(late[d])
    pieces = [pieces[d] for d in range(4)] + [others[d] for d in range(4)]
    terms = grad_inputs_terms(pos, pieces, weight)
    grad_inputs = lax.all_to_all(terms.reshape(8, 64, 384), "z", 0, 0).sum(axis=0).astype(BF)

    own, *sends = relay(own, got)
    pieces, own = lax.optimization_barrier((pieces, own))
    grad_weight = grad_weight_of(pos, gathered, pieces)
    got = [get(v, 4 - d, True) for v, d in zip(sends, STEPS)]
    return finish(own, got), grad_inputs, grad_weight


def solution(mesh):
    fine = Mesh(mesh.devices.reshape(4, 4, 2, 8), ("x", "y", "core", "z"))
    placed = (P("z", ROWS), P(ROWS, "z"), P(ROWS, "z"))
    return jax.shard_map(
        body,
        mesh=fine,
        in_specs=placed,
        out_specs=(P(ROWS, "z"), P("z", ROWS), P(ROWS, "z")),
        check_vma=False,
    )
```
